32 devices in a mesh: dir: 4 (over y, x), adj: 8 (over z, core).
Axes of the slice: x: 2, y: 2, z: 4, core: 2. Of those that a mesh axis runs over, the one named last changes fastest.
Arguments:
- direct_snapshots: bfloat16 [4096, 4096], P('dir', 'adj'), may hold values from -6 to 6
- adjoint_snapshots: bfloat16 [4096, 4096], P('dir', 'adj'), may hold values from -6 to 6
- start_seeds: int32 [512], replicated, may hold values from 0 to 65520
Outputs:
- balancing_modes: float32 [4096, 512], P(('dir', 'adj'))
- adjoint_modes: float32 [4096, 512], P(('dir', 'adj'))
The draws below stay inside these ranges and needn't reach their ends.
All inputs are finite; a program needn't handle non-finite values.
Results may differ from the reference program's by a relative error of at most 0.0019.
Values may be sent and summed in bfloat16 or wider, within the bound.
A program may use at most 128 MiB of HBM per device.

```python
import jax
import jax.numpy as jnp
from jax import lax

M = 4096
P_SIZE = 4096
R = 512
ITERS = 2
N = 4096


def with_ends(drawn, rng, least, top_value):
    extent = drawn.shape
    place = [jax.random.randint(jax.random.fold_in(rng, axis), (), 0, extent[axis]) for axis in range(len(extent))]
    drawn = drawn.at[tuple(place)].set(least)
    longest = extent.index(max(extent))
    place[longest] = (place[longest] + 1) % extent[longest]
    return drawn.at[tuple(place)].set(top_value)


def levels(own_key, dims, cuts, low, largest):
    level = 1.0
    for position, blocks in cuts:
        steps = jax.random.uniform(jax.random.fold_in(jax.random.fold_in(own_key, 6), position), (blocks,), jnp.float32, low / len(cuts), largest / len(cuts))
        level = level * jnp.repeat(jnp.exp(steps), dims[position] // blocks).reshape((-1,) + (1,) * (len(dims) - 1 - position))
    return level


def normal_values(own_key, dims, scale, limit, pieces=(), kind=jnp.bfloat16):
    drawn = scale * jax.random.normal(own_key, dims, jnp.float32)
    if pieces:
        drawn = drawn * levels(own_key, dims, pieces, -0.22, 0.18)
    return jnp.clip(drawn, -limit, limit).astype(kind)


def setup_inputs(seed: int = 0) -> dict:
    key_list = jax.random.split(jax.random.key(seed), 4)
    return {
        "direct_snapshots": normal_values(key_list[0], (N, M), 1.0, 6.0, ((0, 4), (1, 8))),
        "adjoint_snapshots": normal_values(key_list[1], (N, P_SIZE), 1.0, 6.0, ((0, 4), (1, 8))),
        "start_seeds": with_ends(jax.random.randint(key_list[2], (R,), 0, 65521), jax.random.fold_in(key_list[2], 1), 0, 65520).astype(jnp.int32),
    }


def start_block(start_seeds, row_ids):
    row_col = row_ids[:, None]
    seed_row = start_seeds[None, :]
    col_ids = jnp.arange(start_seeds.shape[0], dtype=jnp.int32)[None, :] + 1
    column_term = (row_col + 1) * (col_ids * col_ids % 65521) % 65521
    hashed = (row_col * row_col % 65521 * (seed_row % 997 + 1) + 31 * seed_row + 7 * row_col + column_term) % 65521
    return hashed.astype(jnp.float32) / 65521.0 - 0.5

def orthonormal(raw_block):
    gram_matrix = jnp.dot(raw_block.T.astype(jnp.float32), raw_block.astype(jnp.float32), precision=lax.Precision.HIGHEST, preferred_element_type=jnp.float32)
    factor = jnp.linalg.cholesky(gram_matrix)
    return lax.linalg.triangular_solve(factor, raw_block, left_side=False, lower=True, transpose_a=True)

def reference(direct_snapshots, adjoint_snapshots, start_seeds):
    hankel = jnp.dot(adjoint_snapshots.T.astype(jnp.float32), direct_snapshots.astype(jnp.float32), preferred_element_type=jnp.float32)
    right_basis = start_block(start_seeds, jnp.arange(M, dtype=jnp.int32))
    left_basis = jnp.zeros((P_SIZE, R), jnp.float32)
    for sweep in range(ITERS):
        left_basis = orthonormal(jnp.dot(hankel.astype(jnp.float32), right_basis.astype(jnp.float32), precision=lax.Precision.HIGHEST, preferred_element_type=jnp.float32))
        right_basis = orthonormal(jnp.dot(hankel.T.astype(jnp.float32), left_basis.astype(jnp.float32), precision=lax.Precision.HIGHEST, preferred_element_type=jnp.float32))
    balancing_modes = jnp.dot(direct_snapshots.astype(jnp.float32), right_basis.astype(jnp.bfloat16).astype(jnp.float32), preferred_element_type=jnp.float32)
    adjoint_modes = jnp.dot(adjoint_snapshots.astype(jnp.float32), left_basis.astype(jnp.bfloat16).astype(jnp.float32), preferred_element_type=jnp.float32)
    return (balancing_modes, adjoint_modes)
```

```python
import functools

import jax
import jax.numpy as jnp
from jax import lax
from jax.experimental import pallas as pl
from jax.experimental.pallas import tpu as pltpu
from jax.sharding import PartitionSpec as P

ITERS = 2
CHUNKS = 1
BLOCK = 128


def start_block(start_seeds, offset, length):
    row_col = (offset + jnp.arange(length, dtype=jnp.int32))[:, None]
    seed_row = start_seeds[None, :]
    col_ids = jnp.arange(start_seeds.shape[0], dtype=jnp.int32)[None, :] + 1
    column_term = (row_col + 1) * (col_ids * col_ids % 65521) % 65521
    hashed = (
        row_col * row_col % 65521 * (seed_row % 997 + 1) + 31 * seed_row + 7 * row_col + column_term
    ) % 65521
    return hashed.astype(jnp.float32) / 65521.0 - 0.5


def dot_t(a, b, dims, precision):
    return lax.dot_general(
        a, b, (dims, ((), ())), precision=precision, preferred_element_type=jnp.float32
    )


def invert_block(block):
    size = block.shape[0]
    lane = lax.broadcasted_iota(jnp.int32, (1, size), 1)
    lanes = lax.broadcasted_iota(jnp.int32, (size, size), 1)
    rows = lax.broadcasted_iota(jnp.int32, (size, size), 0)
    state = block
    done = []
    pivots = []
    for step in range(size):
        base = step // 8 * 8
        local_row = step - base
        pivot = state[local_row : local_row + 1, step : step + 1]
        row = state[local_row : local_row + 1, :]
        column = state[:, step : step + 1]
        scaled = jnp.where(lane == step, 1.0, row) * (1.0 / pivot)
        live_rows = rows[base:, :]
        below = live_rows > step
        kept = jnp.where(lane == step, 0.0, state)
        fresh = kept - column * scaled
        if local_row == 7:
            unit = jnp.where(lane == step, 1.0, row)
            top = jnp.concatenate([state[:7, :], unit], axis=0)
            done.append(top)
            state = fresh[8:, :]
        else:
            unit = jnp.where(lane == step, 1.0, state)
            state = jnp.where(below, fresh, jnp.where(live_rows == step, unit, state))
        pivots.append(pivot)
    return jnp.concatenate(done, axis=0), pivots


def factor_kernel(gram_ref, inverse_ref, work_ref):
    size = gram_ref.shape[0]
    work_ref[...] = gram_ref[...]
    row_ids = lax.broadcasted_iota(jnp.int32, (size, size), 0)
    col_ids = lax.broadcasted_iota(jnp.int32, (size, size), 1)
    inverse_ref[...] = jnp.where(row_ids == col_ids, 1.0, 0.0)

    @pl.loop(0, size // BLOCK)
    def _(index):
        start = pl.multiple_of(index * BLOCK, BLOCK)
        span = pl.ds(start, BLOCK)
        eliminated, pivots = invert_block(work_ref[span, span])
        block_rows = lax.broadcasted_iota(jnp.int32, (BLOCK, BLOCK), 0)
        block_cols = lax.broadcasted_iota(jnp.int32, (BLOCK, BLOCK), 1)
        scale = lax.rsqrt(jnp.concatenate(pivots, axis=0))
        inverse = jnp.where(block_rows >= block_cols, eliminated * scale, 0.0)
        high = lax.Precision.HIGHEST
        panel = dot_t(work_ref[:, span], inverse, ((1,), (1,)), high)
        panel_rows = lax.broadcasted_iota(jnp.int32, (size, BLOCK), 0)
        panel = jnp.where(panel_rows >= start + BLOCK, panel, 0.0)
        own = dot_t(inverse, inverse_ref[span, :], ((1,), (0,)), high)
        inverse_ref[span, :] = own
        inverse_ref[...] -= dot_t(panel, own, ((1,), (0,)), high)
        work_ref[...] -= dot_t(panel, panel, ((1,), (1,)), high)


def factor_inverse(gram_matrix):
    shape = jax.ShapeDtypeStruct(gram_matrix.shape, jnp.float32)
    return pl.pallas_call(
        factor_kernel,
        out_shape=shape,
        in_specs=[pl.BlockSpec(memory_space=pltpu.VMEM)],
        out_specs=pl.BlockSpec(memory_space=pltpu.VMEM),
        scratch_shapes=[pltpu.VMEM(gram_matrix.shape, jnp.float32)],
        compiler_params=pltpu.CompilerParams(vmem_limit_bytes=40 * 1024 * 1024),
        name="cholesky_inverse",
    )(gram_matrix)


def gram_of(block_rows):
    return dot_t(block_rows, block_rows, ((0,), (0,)), lax.Precision.HIGHEST)


def product(matrix, block_rows):
    return dot_t(matrix, block_rows, ((1,), (0,)), lax.Precision.HIGH)


def product_back(matrix, block_rows):
    return dot_t(matrix, block_rows, ((0,), (0,)), lax.Precision.HIGH)


def normalize(block_rows, inverse):
    return dot_t(block_rows, inverse, ((1,), (1,)), lax.Precision.HIGH)


def both(products, gram_matrix, axis):
    length = products.shape[0]
    summed = lax.psum(jnp.concatenate([products, gram_matrix], axis=0), axis)
    return summed[:length], summed[length:]


def local(direct_snapshots, adjoint_snapshots, start_seeds):
    adj_count = lax.axis_size("adj")
    adj_index = lax.axis_index("adj")
    share_rows = direct_snapshots.shape[0] // adj_count
    rank = start_seeds.shape[0]
    width = adjoint_snapshots.shape[1] // CHUNKS
    gathered = []
    tiles = []
    for chunk in range(CHUNKS):
        part = lax.all_gather(
            adjoint_snapshots[:, chunk * width : (chunk + 1) * width], "adj", axis=1, tiled=True
        )
        gathered.append(part)
        tile = dot_t(part, direct_snapshots, ((0,), (0,)), None)
        tiles.append(lax.psum_scatter(tile, "dir", scatter_dimension=0, tiled=True))
    hankel_tile = jnp.concatenate(tiles, axis=0)
    right_raw = start_block(
        start_seeds, adj_index * direct_snapshots.shape[1], direct_snapshots.shape[1]
    )
    left_raw = lax.psum(product(hankel_tile, right_raw), "adj")
    for sweep in range(ITERS):
        if sweep:
            left_next, right_gram = both(
                product(hankel_tile, right_raw), gram_of(right_raw), "adj"
            )
            left_raw = normalize(left_next, factor_inverse(right_gram))
        right_next, left_gram = both(
            product_back(hankel_tile, left_raw), gram_of(left_raw), "dir"
        )
        left_inverse = factor_inverse(left_gram)
        right_raw = normalize(right_next, left_inverse)
    left_coarse = normalize(left_raw, left_inverse).astype(jnp.bfloat16)
    left_whole = lax.all_gather(
        left_coarse.reshape(CHUNKS, -1, rank), "dir", axis=1, tiled=True
    ).reshape(-1, rank)
    right_gram = lax.psum(gram_of(right_raw), "adj")
    right_coarse = normalize(right_raw, factor_inverse(right_gram)).astype(jnp.bfloat16)
    balancing_modes = lax.psum_scatter(
        jnp.dot(direct_snapshots, right_coarse, preferred_element_type=jnp.float32),
        "adj",
        scatter_dimension=0,
        tiled=True,
    )
    own_rows = jnp.concatenate(
        [
            lax.dynamic_slice_in_dim(part, adj_index * share_rows, share_rows, 0)
            for part in gathered
        ],
        axis=1,
    )
    adjoint_modes = jnp.dot(own_rows, left_whole, preferred_element_type=jnp.float32)
    return (balancing_modes, adjoint_modes)


def solution(mesh):
    placed = (P("dir", "adj"), P("dir", "adj"), P())
    return jax.shard_map(
        local,
        mesh=mesh,
        in_specs=placed,
        out_specs=(P(("dir", "adj"), None), P(("dir", "adj"), None)),
        check_vma=False,
    )
```

```python
import jax
import jax.numpy as jnp
from jax import lax
from jax.experimental import pallas as pl
from jax.experimental.pallas import tpu as pltpu
from jax.sharding import PartitionSpec as P

ITERS = 2
BLOCK = 128


def start_block(start_seeds, offset, length):
    row_col = (offset + jnp.arange(length, dtype=jnp.int32))[:, None]
    seed_row = start_seeds[None, :]
    col_ids = jnp.arange(start_seeds.shape[0], dtype=jnp.int32)[None, :] + 1
    column_term = (row_col + 1) * (col_ids * col_ids % 65521) % 65521
    hashed = (
        row_col * row_col % 65521 * (seed_row % 997 + 1) + 31 * seed_row + 7 * row_col + column_term
    ) % 65521
    return hashed.astype(jnp.float32) / 65521.0 - 0.5


def dot_t(a, b, dims, precision):
    return lax.dot_general(
        a, b, (dims, ((), ())), precision=precision, preferred_element_type=jnp.float32
    )


def invert_block(block):
    size = block.shape[0]
    lane = lax.broadcasted_iota(jnp.int32, (1, size), 1)
    lanes = lax.broadcasted_iota(jnp.int32, (size, size), 1)
    rows = lax.broadcasted_iota(jnp.int32, (size, size), 0)
    state = block
    done = []
    pivots = []
    for step in range(size):
        base = step // 8 * 8
        local_row = step - base
        pivot = state[local_row : local_row + 1, step : step + 1]
        row = state[local_row : local_row + 1, :]
        column = state[:, step : step + 1]
        scaled = jnp.where(lane == step, 1.0, row) * (1.0 / pivot)
        live_rows = rows[base:, :]
        below = live_rows > step
        kept = jnp.where(lane == step, 0.0, state)
        fresh = kept - column * scaled
        if local_row == 7:
            unit = jnp.where(lane == step, 1.0, row)
            top = jnp.concatenate([state[:7, :], unit], axis=0)
            done.append(top)
            state = fresh[8:, :]
        else:
            unit = jnp.where(lane == step, 1.0, state)
            state = jnp.where(below, fresh, jnp.where(live_rows == step, unit, state))
        pivots.append(pivot)
    return jnp.concatenate(done, axis=0), pivots


def factor_kernel(gram_ref, inverse_ref, work_ref):
    size = gram_ref.shape[0]
    work_ref[...] = gram_ref[...]
    row_ids = lax.broadcasted_iota(jnp.int32, (size, size), 0)
    col_ids = lax.broadcasted_iota(jnp.int32, (size, size), 1)
    inverse_ref[...] = jnp.where(row_ids == col_ids, 1.0, 0.0)

    @pl.loop(0, size // BLOCK)
    def _(index):
        start = pl.multiple_of(index * BLOCK, BLOCK)
        span = pl.ds(start, BLOCK)
        eliminated, pivots = invert_block(work_ref[span, span])
        block_rows = lax.broadcasted_iota(jnp.int32, (BLOCK, BLOCK), 0)
        block_cols = lax.broadcasted_iota(jnp.int32, (BLOCK, BLOCK), 1)
        scale = lax.rsqrt(jnp.concatenate(pivots, axis=0))
        inverse = jnp.where(block_rows >= block_cols, eliminated * scale, 0.0)
        high = lax.Precision.HIGHEST
        panel = dot_t(work_ref[:, span], inverse, ((1,), (1,)), high)
        panel_rows = lax.broadcasted_iota(jnp.int32, (size, BLOCK), 0)
        panel = jnp.where(panel_rows >= start + BLOCK, panel, 0.0)
        own = dot_t(inverse, inverse_ref[span, :], ((1,), (0,)), high)
        inverse_ref[span, :] = own
        inverse_ref[...] -= dot_t(panel, own, ((1,), (0,)), high)
        work_ref[...] -= dot_t(panel, panel, ((1,), (1,)), high)


def factor_inverse(gram_matrix):
    shape = jax.ShapeDtypeStruct(gram_matrix.shape, jnp.float32)
    return pl.pallas_call(
        factor_kernel,
        out_shape=shape,
        in_specs=[pl.BlockSpec(memory_space=pltpu.VMEM)],
        out_specs=pl.BlockSpec(memory_space=pltpu.VMEM),
        scratch_shapes=[pltpu.VMEM(gram_matrix.shape, jnp.float32)],
        compiler_params=pltpu.CompilerParams(vmem_limit_bytes=40 * 1024 * 1024),
        name="cholesky_inverse",
    )(gram_matrix)


def gram_of(block_rows):
    return dot_t(block_rows, block_rows, ((0,), (0,)), lax.Precision.HIGHEST)


def product(matrix, block_rows):
    return dot_t(matrix, block_rows, ((1,), (0,)), lax.Precision.HIGH)


def product_back(matrix, block_rows):
    return dot_t(matrix, block_rows, ((0,), (0,)), lax.Precision.HIGH)


def normalize(block_rows, inverse):
    return dot_t(block_rows, inverse, ((1,), (1,)), lax.Precision.HIGH)


def both(products, gram_matrix, axis):
    gram_sum, products = lax.optimization_barrier((lax.psum(gram_matrix, axis), products))
    return lax.psum(products, axis), gram_sum


def local(direct_snapshots, adjoint_snapshots, start_seeds):
    adj_count = lax.axis_size("adj")
    adj_index = lax.axis_index("adj")
    share_rows = direct_snapshots.shape[0] // adj_count
    dir_count = lax.axis_size("dir")
    turned = lax.all_to_all(adjoint_snapshots, "dir", split_axis=1, concat_axis=0, tiled=True)
    gathered = lax.all_gather(turned, "adj", axis=1, tiled=True)
    direct_whole = lax.all_gather(direct_snapshots, "dir", axis=0, tiled=True)
    hankel_tile = dot_t(gathered, direct_whole, ((0,), (0,)), None)
    right_raw = start_block(
        start_seeds, adj_index * direct_snapshots.shape[1], direct_snapshots.shape[1]
    )
    left_raw = lax.psum(product(hankel_tile, right_raw), "adj")
    for sweep in range(ITERS):
        if sweep:
            left_next, right_gram = both(
                product(hankel_tile, right_raw), gram_of(right_raw), "adj"
            )
            left_raw = normalize(left_next, factor_inverse(right_gram))
        right_next, left_gram = both(
            product_back(hankel_tile, left_raw), gram_of(left_raw), "dir"
        )
        left_inverse = factor_inverse(left_gram)
        right_raw = normalize(right_next, left_inverse)
    left_coarse = normalize(left_raw, left_inverse).astype(jnp.bfloat16)
    right_gram = lax.psum(gram_of(right_raw), "adj")
    right_gram, left_coarse = lax.optimization_barrier((right_gram, left_coarse))
    own_states = lax.dynamic_index_in_dim(
        gathered.reshape(dir_count, adj_count, share_rows, -1), adj_index, 1, keepdims=False
    )
    adjoint_modes = lax.psum_scatter(
        jnp.dot(
            own_states.reshape(dir_count * share_rows, -1),
            left_coarse,
            preferred_element_type=jnp.float32,
        ),
        "dir",
        scatter_dimension=0,
        tiled=True,
    )
    right_inverse, adjoint_modes = lax.optimization_barrier((factor_inverse(right_gram), adjoint_modes))
    right_coarse = normalize(right_raw, right_inverse).astype(jnp.bfloat16)
    balancing_modes = lax.psum_scatter(
        jnp.dot(direct_snapshots, right_coarse, preferred_element_type=jnp.float32),
        "adj",
        scatter_dimension=0,
        tiled=True,
    )
    return (balancing_modes, adjoint_modes)


def solution(mesh):
    placed = (P("dir", "adj"), P("dir", "adj"), P())
    return jax.shard_map(
        local,
        mesh=mesh,
        in_specs=placed,
        out_specs=(P(("dir", "adj"), None), P(("dir", "adj"), None)),
        check_vma=False,
    )
```

```python
import functools

import jax
import jax.numpy as jnp
from jax import lax
from jax.experimental import pallas as pl
from jax.experimental.pallas import tpu as pltpu
from jax.sharding import PartitionSpec as P

ITERS = 2
BLOCK = 128


def start_block(start_seeds, offset, length):
    row_col = (offset + jnp.arange(length, dtype=jnp.int32))[:, None]
    seed_row = start_seeds[None, :]
    col_ids = jnp.arange(start_seeds.shape[0], dtype=jnp.int32)[None, :] + 1
    column_term = (row_col + 1) * (col_ids * col_ids % 65521) % 65521
    hashed = (
        row_col * row_col % 65521 * (seed_row % 997 + 1) + 31 * seed_row + 7 * row_col + column_term
    ) % 65521
    return hashed.astype(jnp.float32) / 65521.0 - 0.5


def dot_t(a, b, dims, precision):
    return lax.dot_general(
        a, b, (dims, ((), ())), precision=precision, preferred_element_type=jnp.float32
    )


def invert_block(block):
    size = block.shape[0]
    lane = lax.broadcasted_iota(jnp.int32, (1, size), 1)
    lanes = lax.broadcasted_iota(jnp.int32, (size, size), 1)
    rows = lax.broadcasted_iota(jnp.int32, (size, size), 0)
    state = block
    done = []
    pivots = []
    for step in range(size):
        base = step // 8 * 8
        local_row = step - base
        pivot = state[local_row : local_row + 1, step : step + 1]
        row = state[local_row : local_row + 1, :]
        column = state[:, step : step + 1]
        scaled = jnp.where(lane == step, 1.0, row) * (1.0 / pivot)
        live_rows = rows[base:, :]
        below = live_rows > step
        kept = jnp.where(lane == step, 0.0, state)
        fresh = kept - column * scaled
        if local_row == 7:
            unit = jnp.where(lane == step, 1.0, row)
            top = jnp.concatenate([state[:7, :], unit], axis=0)
            done.append(top)
            state = fresh[8:, :]
        else:
            unit = jnp.where(lane == step, 1.0, state)
            state = jnp.where(below, fresh, jnp.where(live_rows == step, unit, state))
        pivots.append(pivot)
    return jnp.concatenate(done, axis=0), pivots


def factor_kernel(gram_ref, inverse_ref, work_ref):
    size = gram_ref.shape[0]
    work_ref[...] = gram_ref[...]
    row_ids = lax.broadcasted_iota(jnp.int32, (size, size), 0)
    col_ids = lax.broadcasted_iota(jnp.int32, (size, size), 1)
    inverse_ref[...] = jnp.where(row_ids == col_ids, 1.0, 0.0)

    @pl.loop(0, size // BLOCK)
    def _(index):
        start = pl.multiple_of(index * BLOCK, BLOCK)
        span = pl.ds(start, BLOCK)
        eliminated, pivots = invert_block(work_ref[span, span])
        block_rows = lax.broadcasted_iota(jnp.int32, (BLOCK, BLOCK), 0)
        block_cols = lax.broadcasted_iota(jnp.int32, (BLOCK, BLOCK), 1)
        scale = lax.rsqrt(jnp.concatenate(pivots, axis=0))
        inverse = jnp.where(block_rows >= block_cols, eliminated * scale, 0.0)
        high = lax.Precision.HIGHEST
        panel = dot_t(work_ref[:, span], inverse, ((1,), (1,)), high)
        panel_rows = lax.broadcasted_iota(jnp.int32, (size, BLOCK), 0)
        panel = jnp.where(panel_rows >= start + BLOCK, panel, 0.0)
        own = dot_t(inverse, inverse_ref[span, :], ((1,), (0,)), high)
        inverse_ref[span, :] = own
        inverse_ref[...] -= dot_t(panel, own, ((1,), (0,)), high)
        work_ref[...] -= dot_t(panel, panel, ((1,), (1,)), high)


def factor_inverse(gram_matrix):
    shape = jax.ShapeDtypeStruct(gram_matrix.shape, jnp.float32)
    return pl.pallas_call(
        factor_kernel,
        out_shape=shape,
        in_specs=[pl.BlockSpec(memory_space=pltpu.VMEM)],
        out_specs=pl.BlockSpec(memory_space=pltpu.VMEM),
        scratch_shapes=[pltpu.VMEM(gram_matrix.shape, jnp.float32)],
        compiler_params=pltpu.CompilerParams(vmem_limit_bytes=40 * 1024 * 1024),
        name="cholesky_inverse",
    )(gram_matrix)


def gram_of(block_rows):
    return dot_t(block_rows, block_rows, ((0,), (0,)), lax.Precision.HIGHEST)


def product(matrix, block_rows):
    return dot_t(matrix, block_rows, ((1,), (0,)), lax.Precision.HIGH)


def product_back(matrix, block_rows):
    return dot_t(matrix, block_rows, ((0,), (0,)), lax.Precision.HIGH)


def normalize(block_rows, inverse):
    return dot_t(block_rows, inverse, ((1,), (1,)), lax.Precision.HIGH)


def sum_kernel(axis, pair, count, x_ref, out_ref, held, work, landed, send_sem, recv_sem):
    dir_index, adj_index = lax.axis_index("dir"), lax.axis_index("adj")
    me = dir_index if axis == "dir" else adj_index
    chips = count // pair
    core, chip = lax.rem(me, pair), me // pair
    length = x_ref.shape[0] // pair
    part = length // chips

    def device(index):
        return (index, adj_index) if axis == "dir" else (dir_index, index)

    others = [lax.rem(chip + away, chips) * pair + core for away in range(1, chips)]
    partner = chip * pair + (1 - core)
    peers = others + ([partner] if pair == 2 else [])
    barrier = pltpu.get_barrier_semaphore()
    for peer in peers:
        pl.semaphore_signal(
            barrier, inc=1, device_id=device(peer), device_id_type=pl.DeviceIdType.MESH
        )
    pl.semaphore_wait(barrier, len(peers))

    def send(source, target, slot, peer):
        copy = pltpu.make_async_remote_copy(
            src_ref=source,
            dst_ref=target,
            send_sem=send_sem.at[slot],
            recv_sem=recv_sem.at[slot],
            device_id=device(peer),
            device_id_type=pl.DeviceIdType.MESH,
        )
        copy.start()
        return copy

    own_half = pl.ds(pl.multiple_of(core * length, 8), length)
    if pair == 2:
        other_half = pl.ds(pl.multiple_of((1 - core) * length, 8), length)
        send(x_ref.at[other_half], held, 0, partner).wait()
        work[...] = x_ref[own_half, :] + held[...]
    else:
        work[...] = x_ref[...]
    copies = []
    for away, peer in enumerate(others, 1):
        rows = pl.ds(pl.multiple_of(lax.rem(chip + away, chips) * part, 8), part)
        copies.append(send(work.at[rows], landed.at[away - 1], away, peer))
    total = work[pl.ds(pl.multiple_of(chip * part, 8), part), :]
    for away, copy in enumerate(copies):
        copy.wait()
        total = total + landed[away]
    own_part = pl.ds(pl.multiple_of(core * length + chip * part, 8), part)
    out_ref[own_part, :] = total
    copies = [
        send(out_ref.at[own_part], out_ref.at[own_part], chips + away, peer)
        for away, peer in enumerate(others)
    ]
    for copy in copies:
        copy.wait()
    if pair == 2:
        send(out_ref.at[own_half], out_ref.at[own_half], 2 * chips, partner).wait()


def sum_over(value, axis):
    count = lax.axis_size(axis)
    pair = 2 if axis == "adj" else 1
    rows, columns = value.shape
    chips = count // pair
    held_rows = rows // pair if pair == 2 else 8
    return pl.pallas_call(
        functools.partial(sum_kernel, axis, pair, count),
        out_shape=jax.ShapeDtypeStruct(value.shape, jnp.float32),
        in_specs=[pl.BlockSpec(memory_space=pltpu.VMEM)],
        out_specs=pl.BlockSpec(memory_space=pltpu.VMEM),
        scratch_shapes=[
            pltpu.VMEM((held_rows, columns), jnp.float32),
            pltpu.VMEM((rows // pair, columns), jnp.float32),
            pltpu.VMEM((chips - 1, rows // pair // chips, columns), jnp.float32),
            pltpu.SemaphoreType.DMA((2 * chips + 1,)),
            pltpu.SemaphoreType.DMA((2 * chips + 1,)),
        ],
        compiler_params=pltpu.CompilerParams(
            collective_id=1 if axis == "dir" else 2, vmem_limit_bytes=40 * 1024 * 1024
        ),
        name="gram_sum_" + axis,
    )(value)


def both(products, gram_matrix, axis):
    gram_sum, products = lax.optimization_barrier((sum_over(gram_matrix, axis), products))
    return lax.psum(products, axis), gram_sum


def local(direct_snapshots, adjoint_snapshots, start_seeds):
    adj_count = lax.axis_size("adj")
    adj_index = lax.axis_index("adj")
    share_rows = direct_snapshots.shape[0] // adj_count
    dir_count = lax.axis_size("dir")
    turned = lax.all_to_all(adjoint_snapshots, "dir", split_axis=1, concat_axis=0, tiled=True)
    gathered = lax.all_gather(turned, "adj", axis=1, tiled=True)
    direct_whole = lax.all_gather(direct_snapshots, "dir", axis=0, tiled=True)
    hankel_tile = dot_t(gathered, direct_whole, ((0,), (0,)), None)
    right_raw = start_block(
        start_seeds, adj_index * direct_snapshots.shape[1], direct_snapshots.shape[1]
    )
    left_raw = lax.psum(product(hankel_tile, right_raw), "adj")
    for sweep in range(ITERS):
        if sweep:
            left_next, right_gram = both(
                product(hankel_tile, right_raw), gram_of(right_raw), "adj"
            )
            left_raw = normalize(left_next, factor_inverse(right_gram))
        right_next, left_gram = both(
            product_back(hankel_tile, left_raw), gram_of(left_raw), "dir"
        )
        left_inverse = factor_inverse(left_gram)
        right_raw = normalize(right_next, left_inverse)
    left_coarse = normalize(left_raw, left_inverse).astype(jnp.bfloat16)
    right_gram = sum_over(gram_of(right_raw), "adj")
    right_gram, left_coarse = lax.optimization_barrier((right_gram, left_coarse))
    own_states = lax.dynamic_index_in_dim(
        gathered.reshape(dir_count, adj_count, share_rows, -1), adj_index, 1, keepdims=False
    )
    adjoint_modes = lax.psum_scatter(
        jnp.dot(
            own_states.reshape(dir_count * share_rows, -1),
            left_coarse,
            preferred_element_type=jnp.float32,
        ),
        "dir",
        scatter_dimension=0,
        tiled=True,
    )
    right_inverse, adjoint_modes = lax.optimization_barrier((factor_inverse(right_gram), adjoint_modes))
    right_coarse = normalize(right_raw, right_inverse).astype(jnp.bfloat16)
    balancing_modes = lax.psum_scatter(
        jnp.dot(direct_snapshots, right_coarse, preferred_element_type=jnp.float32),
        "adj",
        scatter_dimension=0,
        tiled=True,
    )
    return (balancing_modes, adjoint_modes)


def solution(mesh):
    placed = (P("dir", "adj"), P("dir", "adj"), P())
    return jax.shard_map(
        local,
        mesh=mesh,
        in_specs=placed,
        out_specs=(P(("dir", "adj"), None), P(("dir", "adj"), None)),
        check_vma=False,
    )
```

```python
import functools

import jax
import jax.numpy as jnp
from jax import lax
from jax.experimental import pallas as pl
from jax.experimental.pallas import tpu as pltpu
from jax.sharding import PartitionSpec as P

ITERS = 2
BLOCK = 128


def start_block(start_seeds, offset, length):
    row_col = (offset + jnp.arange(length, dtype=jnp.int32))[:, None]
    seed_row = start_seeds[None, :]
    col_ids = jnp.arange(start_seeds.shape[0], dtype=jnp.int32)[None, :] + 1
    column_term = (row_col + 1) * (col_ids * col_ids % 65521) % 65521
    hashed = (
        row_col * row_col % 65521 * (seed_row % 997 + 1) + 31 * seed_row + 7 * row_col + column_term
    ) % 65521
    return hashed.astype(jnp.float32) / 65521.0 - 0.5


def dot_t(a, b, dims, precision):
    return lax.dot_general(
        a, b, (dims, ((), ())), precision=precision, preferred_element_type=jnp.float32
    )


def invert_block(block):
    size = block.shape[0]
    lane = lax.broadcasted_iota(jnp.int32, (1, size), 1)
    lanes = lax.broadcasted_iota(jnp.int32, (size, size), 1)
    rows = lax.broadcasted_iota(jnp.int32, (size, size), 0)
    state = block
    done = []
    pivots = []
    for step in range(size):
        base = step // 8 * 8
        local_row = step - base
        pivot = state[local_row : local_row + 1, step : step + 1]
        row = state[local_row : local_row + 1, :]
        column = state[:, step : step + 1]
        scaled = jnp.where(lane == step, 1.0, row) * (1.0 / pivot)
        live_rows = rows[base:, :]
        below = live_rows > step
        kept = jnp.where(lane == step, 0.0, state)
        fresh = kept - column * scaled
        if local_row == 7:
            unit = jnp.where(lane == step, 1.0, row)
            top = jnp.concatenate([state[:7, :], unit], axis=0)
            done.append(top)
            state = fresh[8:, :]
        else:
            unit = jnp.where(lane == step, 1.0, state)
            state = jnp.where(below, fresh, jnp.where(live_rows == step, unit, state))
        pivots.append(pivot)
    return jnp.concatenate(done, axis=0), pivots


def factor_kernel(gram_ref, inverse_ref, work_ref):
    size = gram_ref.shape[0]
    work_ref[...] = gram_ref[...]
    row_ids = lax.broadcasted_iota(jnp.int32, (size, size), 0)
    col_ids = lax.broadcasted_iota(jnp.int32, (size, size), 1)
    inverse_ref[...] = jnp.where(row_ids == col_ids, 1.0, 0.0)

    @pl.loop(0, size // BLOCK)
    def _(index):
        start = pl.multiple_of(index * BLOCK, BLOCK)
        span = pl.ds(start, BLOCK)
        eliminated, pivots = invert_block(work_ref[span, span])
        block_rows = lax.broadcasted_iota(jnp.int32, (BLOCK, BLOCK), 0)
        block_cols = lax.broadcasted_iota(jnp.int32, (BLOCK, BLOCK), 1)
        scale = lax.rsqrt(jnp.concatenate(pivots, axis=0))
        inverse = jnp.where(block_rows >= block_cols, eliminated * scale, 0.0)
        high = lax.Precision.HIGHEST
        panel = dot_t(work_ref[:, span], inverse, ((1,), (1,)), high)
        panel_rows = lax.broadcasted_iota(jnp.int32, (size, BLOCK), 0)
        panel = jnp.where(panel_rows >= start + BLOCK, panel, 0.0)
        own = dot_t(inverse, inverse_ref[span, :], ((1,), (0,)), high)
        inverse_ref[span, :] = own
        inverse_ref[...] -= dot_t(panel, own, ((1,), (0,)), high)
        work_ref[...] -= dot_t(panel, panel, ((1,), (1,)), high)


def factor_inverse(gram_matrix):
    shape = jax.ShapeDtypeStruct(gram_matrix.shape, jnp.float32)
    return pl.pallas_call(
        factor_kernel,
        out_shape=shape,
        in_specs=[pl.BlockSpec(memory_space=pltpu.VMEM)],
        out_specs=pl.BlockSpec(memory_space=pltpu.VMEM),
        scratch_shapes=[pltpu.VMEM(gram_matrix.shape, jnp.float32)],
        compiler_params=pltpu.CompilerParams(vmem_limit_bytes=40 * 1024 * 1024),
        name="cholesky_inverse",
    )(gram_matrix)


def gram_of(block_rows):
    return dot_t(block_rows, block_rows, ((0,), (0,)), lax.Precision.HIGHEST)


def product(matrix, block_rows):
    return dot_t(matrix, block_rows, ((1,), (0,)), lax.Precision.HIGH)


def product_back(matrix, block_rows):
    return dot_t(matrix, block_rows, ((0,), (0,)), lax.Precision.HIGH)


def normalize(block_rows, inverse):
    return dot_t(block_rows, inverse, ((1,), (1,)), lax.Precision.HIGH)


def sum_kernel(axis, pair, count, x_ref, out_ref, held, work, landed, send_sem, recv_sem):
    dir_index, adj_index = lax.axis_index("dir"), lax.axis_index("adj")
    me = dir_index if axis == "dir" else adj_index
    chips = count // pair
    core, chip = lax.rem(me, pair), me // pair
    length = x_ref.shape[0] // pair
    part = length // chips

    def device(index):
        return (index, adj_index) if axis == "dir" else (dir_index, index)

    others = [lax.rem(chip + away, chips) * pair + core for away in range(1, chips)]
    partner = chip * pair + (1 - core)
    peers = others + ([partner] if pair == 2 else [])
    barrier = pltpu.get_barrier_semaphore()
    for peer in peers:
        pl.semaphore_signal(
            barrier, inc=1, device_id=device(peer), device_id_type=pl.DeviceIdType.MESH
        )
    pl.semaphore_wait(barrier, len(peers))

    def send(source, target, slot, peer):
        copy = pltpu.make_async_remote_copy(
            src_ref=source,
            dst_ref=target,
            send_sem=send_sem.at[slot],
            recv_sem=recv_sem.at[slot],
            device_id=device(peer),
            device_id_type=pl.DeviceIdType.MESH,
        )
        copy.start()
        return copy

    own_half = pl.ds(pl.multiple_of(core * length, 8), length)
    if pair == 2:
        other_half = pl.ds(pl.multiple_of((1 - core) * length, 8), length)
        send(x_ref.at[other_half], held, 0, partner).wait()
        work[...] = x_ref[own_half, :] + held[...]
    else:
        work[...] = x_ref[...]
    copies = []
    for away, peer in enumerate(others, 1):
        rows = pl.ds(pl.multiple_of(lax.rem(chip + away, chips) * part, 8), part)
        copies.append(send(work.at[rows], landed.at[away - 1], away, peer))
    total = work[pl.ds(pl.multiple_of(chip * part, 8), part), :]
    for away, copy in enumerate(copies):
        copy.wait()
        total = total + landed[away]
    own_part = pl.ds(pl.multiple_of(core * length + chip * part, 8), part)
    out_ref[own_part, :] = total
    copies = [
        send(out_ref.at[own_part], out_ref.at[own_part], chips + away, peer)
        for away, peer in enumerate(others)
    ]
    for copy in copies:
        copy.wait()
    if pair == 2:
        send(out_ref.at[own_half], out_ref.at[own_half], 2 * chips, partner).wait()


def gather_kernel(count, x_ref, out_ref, local_sem, send_sem, recv_sem):
    me, adj_index = lax.axis_index("dir"), lax.axis_index("adj")
    length = x_ref.shape[0]
    peers = [lax.rem(me + away, count) for away in range(1, count)]
    barrier = pltpu.get_barrier_semaphore()
    for peer in peers:
        pl.semaphore_signal(
            barrier, inc=1, device_id=(peer, adj_index), device_id_type=pl.DeviceIdType.MESH
        )
    pl.semaphore_wait(barrier, len(peers))
    own = out_ref.at[pl.ds(pl.multiple_of(me * length, 16), length)]
    copies = [
        pltpu.make_async_remote_copy(
            src_ref=x_ref,
            dst_ref=own,
            send_sem=send_sem.at[slot],
            recv_sem=recv_sem.at[slot],
            device_id=(peer, adj_index),
            device_id_type=pl.DeviceIdType.MESH,
        )
        for slot, peer in enumerate(peers)
    ]
    for copy in copies:
        copy.start()
    kept = pltpu.make_async_copy(x_ref, own, local_sem)
    kept.start()
    kept.wait()
    for copy in copies:
        copy.wait()


def gather_dir(value):
    count = lax.axis_size("dir")
    rows, columns = value.shape
    return pl.pallas_call(
        functools.partial(gather_kernel, count),
        out_shape=jax.ShapeDtypeStruct((rows * count, columns), value.dtype),
        in_specs=[pl.BlockSpec(memory_space=pl.ANY)],
        out_specs=pl.BlockSpec(memory_space=pl.ANY),
        scratch_shapes=[
            pltpu.SemaphoreType.DMA(()),
            pltpu.SemaphoreType.DMA((count - 1,)),
            pltpu.SemaphoreType.DMA((count - 1,)),
        ],
        compiler_params=pltpu.CompilerParams(collective_id=3),
        name="gather_dir",
    )(value)


def sum_over(value, axis):
    count = lax.axis_size(axis)
    pair = 2 if axis == "adj" else 1
    rows, columns = value.shape
    chips = count // pair
    held_rows = rows // pair if pair == 2 else 8
    return pl.pallas_call(
        functools.partial(sum_kernel, axis, pair, count),
        out_shape=jax.ShapeDtypeStruct(value.shape, jnp.float32),
        in_specs=[pl.BlockSpec(memory_space=pltpu.VMEM)],
        out_specs=pl.BlockSpec(memory_space=pltpu.VMEM),
        scratch_shapes=[
            pltpu.VMEM((held_rows, columns), jnp.float32),
            pltpu.VMEM((rows // pair, columns), jnp.float32),
            pltpu.VMEM((chips - 1, rows // pair // chips, columns), jnp.float32),
            pltpu.SemaphoreType.DMA((2 * chips + 1,)),
            pltpu.SemaphoreType.DMA((2 * chips + 1,)),
        ],
        compiler_params=pltpu.CompilerParams(
            collective_id=1 if axis == "dir" else 2, vmem_limit_bytes=40 * 1024 * 1024
        ),
        name="gram_sum_" + axis,
    )(value)


def both(products, gram_matrix, axis):
    gram_sum, products = lax.optimization_barrier((sum_over(gram_matrix, axis), products))
    return lax.psum(products, axis), gram_sum


def local(direct_snapshots, adjoint_snapshots, start_seeds):
    adj_count = lax.axis_size("adj")
    adj_index = lax.axis_index("adj")
    share_rows = direct_snapshots.shape[0] // adj_count
    dir_count = lax.axis_size("dir")
    turned = lax.all_to_all(adjoint_snapshots, "dir", split_axis=1, concat_axis=0, tiled=True)
    turned, direct_later = lax.optimization_barrier((turned, direct_snapshots))
    gathered = lax.all_gather(turned, "adj", axis=1, tiled=True)
    direct_whole = gather_dir(direct_later)
    hankel_tile = dot_t(gathered, direct_whole, ((0,), (0,)), None)
    right_raw = start_block(
        start_seeds, adj_index * direct_snapshots.shape[1], direct_snapshots.shape[1]
    )
    left_raw = lax.psum(product(hankel_tile, right_raw), "adj")
    for sweep in range(ITERS):
        if sweep:
            left_next, right_gram = both(
                product(hankel_tile, right_raw), gram_of(right_raw), "adj"
            )
            left_raw = normalize(left_next, factor_inverse(right_gram))
        right_next, left_gram = both(
            product_back(hankel_tile, left_raw), gram_of(left_raw), "dir"
        )
        left_inverse = factor_inverse(left_gram)
        right_raw = normalize(right_next, left_inverse)
    left_coarse = normalize(left_raw, left_inverse).astype(jnp.bfloat16)
    right_gram = sum_over(gram_of(right_raw), "adj")
    right_gram, left_coarse = lax.optimization_barrier((right_gram, left_coarse))
    own_states = lax.dynamic_index_in_dim(
        gathered.reshape(dir_count, adj_count, share_rows, -1), adj_index, 1, keepdims=False
    )
    adjoint_modes = lax.psum_scatter(
        jnp.dot(
            own_states.reshape(dir_count * share_rows, -1),
            left_coarse,
            preferred_element_type=jnp.float32,
        ),
        "dir",
        scatter_dimension=0,
        tiled=True,
    )
    right_inverse, adjoint_modes = lax.optimization_barrier((factor_inverse(right_gram), adjoint_modes))
    right_coarse = normalize(right_raw, right_inverse).astype(jnp.bfloat16)
    balancing_modes = lax.psum_scatter(
        jnp.dot(direct_snapshots, right_coarse, preferred_element_type=jnp.float32),
        "adj",
        scatter_dimension=0,
        tiled=True,
    )
    return (balancing_modes, adjoint_modes)


def solution(mesh):
    placed = (P("dir", "adj"), P("dir", "adj"), P())
    return jax.shard_map(
        local,
        mesh=mesh,
        in_specs=placed,
        out_specs=(P(("dir", "adj"), None), P(("dir", "adj"), None)),
        check_vma=False,
    )
```
